32 devices in a mesh: chan: 8 (over y, x, core), tm: 4 (over z).
Axes of the slice: x: 2, y: 2, z: 4, core: 2. Of those that a mesh axis runs over, the one named last changes fastest.
Arguments:
- raw_strain: float32 [512, 4096], P('chan', 'tm'), may hold values from -2000 to 2000
- fir_taps: float32 [64], replicated, may hold values from -0.75 to 0.75
- block_mask: int32 [8, 8], replicated, may hold values 0 or 1
Outputs:
- correlations: float32 [128, 512, 512], P('tm', 'chan')
The draws below stay inside these ranges and needn't reach their ends.
All inputs are finite; a program needn't handle non-finite values.
Results may differ from the reference program's by a relative error of at most 0.0054.
Values may be sent and summed in bfloat16 or wider, within the bound.
A program may use at most 64 MiB of HBM per device.

```python
import math
import jax
import jax.numpy as jnp
from jax import lax

CHAN_DEV = 64
DECIM = 8
TAPS = 64
LAGS = 128
CHANNELS = 512
BLOCKS = 8
SAMPLES = 512
RAW = 4096


def draw_raw_strain(key, part):
    key_scale, key_noise = jax.random.split(key, 2)
    channel_scale = jnp.exp(jax.random.uniform(key_scale, (CHANNELS, 1), jnp.float32) * math.log(10.0))
    position = jnp.arange(RAW, dtype=jnp.float32)[None, :] / RAW
    base = jnp.clip(jax.random.normal(key_noise, (CHANNELS, RAW), jnp.float32), -6.0, 6.0)
    envelope = jnp.exp(math.log(10.0) * position)
    return (channel_scale * envelope * base).astype(jnp.float32)


def with_ends(entries, rng, least, largest):
    longest = entries.shape.index(max(entries.shape))
    spots = []
    for shift in (0, 1):
        where = [jax.random.randint(jax.random.fold_in(rng, axis), (), 0, length) for axis, length in enumerate(entries.shape)]
        where[longest] = (where[longest] + shift) % entries.shape[longest]
        spots.append(tuple(where))
    return entries.at[spots[0]].set(least).at[spots[1]].set(largest)


def scatter_about(rng, extent, spread, limit, kind=jnp.bfloat16):
    result = jax.random.normal(rng, extent, jnp.float32) * spread
    return jnp.minimum(jnp.maximum(result, -limit), limit).astype(kind)


def setup_inputs(seed: int = 0) -> dict:
    keys = jax.random.split(jax.random.key(seed), 4)
    raw_strain = draw_raw_strain(jax.random.fold_in(keys[3], 71), 0)
    fir_taps = scatter_about(keys[1], (TAPS,), TAPS ** -0.5, 0.75, jnp.float32)
    block_mask = with_ends((jax.random.randint(keys[2], (BLOCKS, BLOCKS), 0, 2) < 1).astype(jnp.int32), jax.random.fold_in(keys[2], 1), 0, 1)
    return dict(raw_strain=raw_strain, fir_taps=fir_taps, block_mask=block_mask)


def reference(raw_strain, fir_taps, block_mask):
    margin = TAPS - DECIM
    padded = jnp.pad(raw_strain, ((0, 0), (margin, 0)))
    decimated = jnp.zeros((CHANNELS, SAMPLES), jnp.float32)
    for tap_index in range(TAPS):
        begin = margin + DECIM - 1 - tap_index
        strided = lax.slice_in_dim(padded, begin, begin + DECIM * (SAMPLES - 1) + 1, DECIM, 1)
        decimated = decimated + fir_taps[tap_index] * strided
    rounded = decimated.astype(jnp.bfloat16)
    float_values = rounded.astype(jnp.float32)
    root_mean = jnp.sqrt(lax.optimization_barrier(jnp.mean(float_values * float_values, axis=1, keepdims=True)) + 1e-06)
    whitened = (float_values / root_mean).astype(jnp.bfloat16)
    wide_values = whitened.astype(jnp.float32)
    wide_padded = jnp.pad(wide_values, ((0, 0), (0, LAGS)))
    mask_full = jnp.repeat(jnp.repeat(block_mask, CHAN_DEV, axis=0), CHAN_DEV, axis=1)
    weights = mask_full.astype(jnp.float32) * (1.0 / math.sqrt(SAMPLES))

    def one_lag(lag_index):
        shifted = lax.dynamic_slice_in_dim(wide_padded, lag_index, SAMPLES, 1)
        product = jnp.dot(wide_values, shifted.T, precision=lax.Precision.HIGHEST, preferred_element_type=jnp.float32)
        return product * weights
    return lax.map(one_lag, jnp.arange(LAGS, dtype=jnp.int32))
```

```python
import functools
import math

import jax
import jax.numpy as jnp
from jax import lax
from jax.experimental import pallas as pl
from jax.experimental.pallas import tpu as pltpu
from jax.sharding import PartitionSpec as P

DECIM = 8
TAPS = 64
LAGS = 128
LANES = 128
WIDE = 2 * LANES
MESH = pl.DeviceIdType.MESH


def filter_tile(taps_ref):
    row = lax.broadcasted_iota(jnp.int32, (DECIM, LANES), 0)
    lane = lax.broadcasted_iota(jnp.int32, (DECIM, LANES), 1)
    which = DECIM * lane + (DECIM - 1) - row
    base = jnp.zeros((DECIM, LANES), jnp.float32)
    for tap in range(TAPS):
        base = jnp.where(which == tap, taps_ref[tap], base)
    rows = [base if m == 0 else pltpu.roll(base, m, 1) for m in range(WIDE // DECIM)]
    return jnp.concatenate(rows, axis=0)


def gather_kernel(
    chans, tms, taps_ref, raw_ref, out_ref,
    raw_v, halo, zbuf, raw_sem, halo_send, halo_recv, z_send, z_recv, c_send, c_recv, s_send, s_recv,
):
    rows, span = raw_v.shape
    outputs = span // DECIM
    samples = outputs * tms
    chips = chans // 2
    c = lax.axis_index("chan")
    z = lax.axis_index("tm")
    chip, core = c // 2, c % 2
    sibling = 2 * chip + (1 - core)

    load = pltpu.make_async_copy(raw_ref, raw_v, raw_sem)
    load.start()

    barrier = pltpu.get_barrier_semaphore()
    z_peers = [lax.rem(z + d, tms) for d in range(1, tms)]
    c_peers = [2 * lax.rem(chip + d, chips) + core for d in range(1, chips)]
    for peer in z_peers:
        pl.semaphore_signal(barrier, inc=1, device_id=(c, peer), device_id_type=MESH)
    for peer in c_peers + [sibling]:
        pl.semaphore_signal(barrier, inc=1, device_id=(peer, z), device_id_type=MESH)

    table = filter_tile(taps_ref)
    load.wait()
    pl.semaphore_wait(barrier, tms - 1 + chips)

    halo_copy = pltpu.make_async_remote_copy(
        src_ref=raw_v.at[:, pl.ds(span - LANES, LANES)],
        dst_ref=halo,
        send_sem=halo_send,
        recv_sem=halo_recv,
        device_id=(c, jnp.minimum(z + 1, tms - 1)),
        device_id_type=MESH,
    )

    @pl.when(z < tms - 1)
    def _():
        halo_copy.start()

    @pl.when(z == 0)
    def _():
        halo[...] = jnp.zeros_like(halo)

    parts = span // WIDE
    stacked = jnp.concatenate([raw_v[:, q * WIDE : (q + 1) * WIDE] for q in range(parts)], axis=0)
    product = jnp.dot(
        stacked, table, precision=lax.Precision.HIGHEST, preferred_element_type=jnp.float32
    )
    step = WIDE // DECIM
    lane = lax.broadcasted_iota(jnp.int32, (rows, LANES), 1)
    total = product[:rows]
    for q in range(1, parts):
        turned = pltpu.roll(product[q * rows : (q + 1) * rows], q * step, 1)
        if q == parts - 1:
            turned = jnp.where(lane < DECIM, 0.0, turned)
        total = total + turned

    @pl.when(z > 0)
    def _():
        halo_copy.wait_recv()

    before = jnp.dot(
        halo[...], table[WIDE - LANES :], precision=lax.Precision.HIGHEST,
        preferred_element_type=jnp.float32,
    )
    before = pltpu.roll(before, LANES - step, 1)
    total = total + jnp.where(lane < DECIM, before, 0.0)
    zbuf[z] = total.astype(jnp.bfloat16)

    z_copies = []
    for d in range(1, tms):
        copy = pltpu.make_async_remote_copy(
            src_ref=zbuf.at[z],
            dst_ref=zbuf.at[z],
            send_sem=z_send.at[d - 1],
            recv_sem=z_recv.at[d - 1],
            device_id=(c, z_peers[d - 1]),
            device_id_type=MESH,
        )
        copy.start()
        z_copies.append(copy)
    for d in range(1, tms):
        source = lax.rem(z - d + tms, tms)
        pltpu.make_async_remote_copy(
            src_ref=zbuf.at[source],
            dst_ref=zbuf.at[source],
            send_sem=z_send.at[d - 1],
            recv_sem=z_recv.at[d - 1],
            device_id=(c, source),
            device_id_type=MESH,
        ).wait_recv()

    squares = jnp.zeros((rows, LANES), jnp.float32)
    for k in range(tms):
        value = zbuf[k].astype(jnp.float32)
        squares = squares + value * value
    root = jnp.sqrt(jnp.sum(squares, axis=1, keepdims=True) * (1.0 / samples) + 1e-06)
    mine = pl.ds(pl.multiple_of(c * rows, rows), rows)
    for k in range(tms):
        out_ref[mine, k * outputs : (k + 1) * outputs] = (
            zbuf[k].astype(jnp.float32) / root
        ).astype(jnp.bfloat16)

    def block(owner):
        return out_ref.at[pl.ds(pl.multiple_of(owner * rows, rows), rows)]

    def push(owner, target, send, recv):
        return pltpu.make_async_remote_copy(
            src_ref=block(owner),
            dst_ref=block(owner),
            send_sem=send,
            recv_sem=recv,
            device_id=(target, z),
            device_id_type=MESH,
        )

    sends = []
    for d in range(1, chips):
        copy = push(c, c_peers[d - 1], c_send.at[d - 1], c_recv.at[d - 1])
        copy.start()
        sends.append(copy)
    copy = push(c, sibling, s_send.at[0], s_recv.at[0])
    copy.start()
    sends.append(copy)
    for d in range(1, chips):
        owner = 2 * lax.rem(chip - d + chips, chips) + core
        push(owner, owner, c_send.at[d - 1], c_recv.at[d - 1]).wait_recv()
        copy = push(owner, sibling, s_send.at[d], s_recv.at[d])
        copy.start()
        sends.append(copy)
    for d in range(chips):
        owner = 2 * lax.rem(chip - d + chips, chips) + (1 - core)
        push(owner, sibling, s_send.at[d], s_recv.at[d]).wait_recv()

    @pl.when(z < tms - 1)
    def _():
        halo_copy.wait_send()

    for copy in z_copies + sends:
        copy.wait_send()


def correlate_kernel(lag_count, per_step, mask_ref, all_ref, out_ref, left):
    channels, samples = all_ref.shape
    rows = out_ref.shape[1]
    c = lax.axis_index("chan")
    first = lax.axis_index("tm") * lag_count + pl.program_id(0) * per_step
    mine = pl.ds(pl.multiple_of(c * rows, rows), rows)
    lane = lax.broadcasted_iota(jnp.int32, (rows, LANES), 1)
    tiles = [
        all_ref[mine, k * LANES : (k + 1) * LANES].astype(jnp.float32)
        for k in range(samples // LANES)
    ]
    for step in range(per_step):
        lag = first + step
        earlier = jnp.zeros((rows, LANES), jnp.float32)
        for k, tile in enumerate(tiles):
            turned = pltpu.roll(tile, lag, 1)
            left[step * rows : (step + 1) * rows, k * LANES : (k + 1) * LANES] = jnp.where(
                lane < lag, earlier, turned
            ).astype(jnp.bfloat16)
            earlier = turned
    wide = min(channels, 512)
    blocks = wide // rows
    column = lax.broadcasted_iota(jnp.int32, (1, wide), 1) // rows

    def one(part, carry):
        at = part * wide
        weight = jnp.zeros((1, wide), jnp.float32)
        for b in range(blocks):
            kept = mask_ref[c, part * blocks + b].astype(jnp.float32) * (1.0 / math.sqrt(samples))
            weight = jnp.where(column == b, kept, weight)
        right = all_ref[pl.ds(pl.multiple_of(at, wide), wide), :]
        product = lax.dot_general(
            left[...], right, (((1,), (1,)), ((), ())), preferred_element_type=jnp.float32
        )
        out_ref[:, :, pl.ds(pl.multiple_of(at, wide), wide)] = (product * weight).reshape(
            per_step, rows, wide
        )
        return carry

    if channels == wide:
        one(0, 0)
    else:
        lax.fori_loop(0, channels // wide, one, 0)


def per_device(raw_strain, fir_taps, block_mask, *, chans, tms):
    rows, span = raw_strain.shape
    outputs = span // DECIM
    samples = outputs * tms
    channels = rows * chans
    chips = chans // 2
    record = pl.pallas_call(
        functools.partial(gather_kernel, chans, tms),
        out_shape=jax.ShapeDtypeStruct((channels, samples), jnp.bfloat16),
        in_specs=[
            pl.BlockSpec(memory_space=pltpu.SMEM),
            pl.BlockSpec(memory_space=pl.ANY),
        ],
        out_specs=pl.BlockSpec(memory_space=pltpu.VMEM),
        scratch_shapes=[
            pltpu.VMEM((rows, span), jnp.float32),
            pltpu.VMEM((rows, LANES), jnp.float32),
            pltpu.VMEM((tms, rows, outputs), jnp.bfloat16),
            pltpu.SemaphoreType.DMA,
            pltpu.SemaphoreType.DMA,
            pltpu.SemaphoreType.DMA,
            pltpu.SemaphoreType.DMA((tms - 1,)),
            pltpu.SemaphoreType.DMA((tms - 1,)),
            pltpu.SemaphoreType.DMA((chips - 1,)),
            pltpu.SemaphoreType.DMA((chips - 1,)),
            pltpu.SemaphoreType.DMA((chips,)),
            pltpu.SemaphoreType.DMA((chips,)),
        ],
        compiler_params=pltpu.CompilerParams(
            collective_id=0, has_side_effects=True, vmem_limit_bytes=24 * 2**20
        ),
        name="gather",
    )(fir_taps, raw_strain)

    lag_count = LAGS // tms
    per_step = min(4, lag_count)
    return pl.pallas_call(
        functools.partial(correlate_kernel, lag_count, per_step),
        grid=(lag_count // per_step,),
        out_shape=jax.ShapeDtypeStruct((lag_count, rows, channels), jnp.float32),
        in_specs=[
            pl.BlockSpec(memory_space=pltpu.SMEM),
            pl.BlockSpec((channels, samples), lambda g: (0, 0)),
        ],
        out_specs=pl.BlockSpec((per_step, rows, channels), lambda g: (g, 0, 0)),
        scratch_shapes=[pltpu.VMEM((per_step * rows, samples), jnp.bfloat16)],
        compiler_params=pltpu.CompilerParams(vmem_limit_bytes=40 * 2**20),
        name="correlate",
    )(block_mask, record)


def solution(mesh):
    placed = (P("chan", "tm"), P(), P())
    return jax.shard_map(
        functools.partial(per_device, chans=mesh.shape["chan"], tms=mesh.shape["tm"]),
        mesh=mesh, in_specs=placed, out_specs=P("tm", "chan", None), check_vma=False,
    )
```

```python
import functools
import math

import jax
import jax.numpy as jnp
from jax import lax
from jax.experimental import pallas as pl
from jax.experimental.pallas import tpu as pltpu
from jax.sharding import PartitionSpec as P

DECIM = 8
TAPS = 64
LAGS = 128
LANES = 128
WIDE = 2 * LANES
MESH = pl.DeviceIdType.MESH


def filter_tile(taps_ref):
    row = lax.broadcasted_iota(jnp.int32, (DECIM, LANES), 0)
    lane = lax.broadcasted_iota(jnp.int32, (DECIM, LANES), 1)
    which = DECIM * lane + (DECIM - 1) - row
    base = jnp.zeros((DECIM, LANES), jnp.float32)
    for tap in range(TAPS):
        base = jnp.where(which == tap, taps_ref[tap], base)
    rows = [base if m == 0 else pltpu.roll(base, m, 1) for m in range(WIDE // DECIM)]
    return jnp.concatenate(rows, axis=0)


def flipped(index, bits):
    place = 1
    while place <= bits:
        if bits & place:
            index = index + place - 2 * place * lax.rem(index // place, 2)
        place *= 2
    return index


def whiten(pieces, samples):
    squares = pieces[0] * pieces[0]
    for piece in pieces[1:]:
        squares = squares + piece * piece
    root = jnp.sqrt(jnp.sum(squares, axis=1, keepdims=True) * (1.0 / samples) + 1e-06)
    return [(piece / root).astype(jnp.bfloat16) for piece in pieces]


def gather_kernel(
    chans, tms, taps_hbm, raw_hbm, mask_hbm, left, right, weight_ref,
    raw_v, taps_ref, mask_ref, halo, record,
    load_sems, halo_send, halo_recv, z_send, z_recv, c_send, c_recv, s_send, s_recv,
):
    rows, span = raw_v.shape
    outputs = span // DECIM
    samples = outputs * tms
    chips = chans // 2
    lag_count = left.shape[0] // rows
    c = lax.axis_index("chan")
    z = lax.axis_index("tm")
    chip, core = c // 2, lax.rem(c, 2)
    sibling = 2 * chip + (1 - core)

    load_raw = pltpu.make_async_copy(raw_hbm, raw_v, load_sems.at[0])
    load_taps = pltpu.make_async_copy(taps_hbm, taps_ref, load_sems.at[1])
    load_mask = pltpu.make_async_copy(mask_hbm, mask_ref, load_sems.at[2])
    load_taps.start()
    load_raw.start()
    load_mask.start()

    z_peers = [
        flipped(z, d) if tms & (tms - 1) == 0 else lax.rem(z + d, tms) for d in range(1, tms)
    ]
    z_sources = [
        flipped(z, d) if tms & (tms - 1) == 0 else lax.rem(z - d + tms, tms)
        for d in range(1, tms)
    ]
    power = chips & (chips - 1) == 0
    c_peers = [
        2 * (flipped(chip, d) if power else lax.rem(chip + d, chips)) + core
        for d in range(1, chips)
    ]
    c_sources = [
        2 * (flipped(chip, d) if power else lax.rem(chip - d + chips, chips)) + core
        for d in range(1, chips)
    ]
    barrier = pltpu.get_barrier_semaphore()
    for peer in z_peers:
        pl.semaphore_signal(barrier, inc=1, device_id=(c, peer), device_id_type=MESH)
    for peer in c_peers + [sibling]:
        pl.semaphore_signal(barrier, inc=1, device_id=(peer, z), device_id_type=MESH)

    load_taps.wait()
    table = filter_tile(taps_ref)
    load_raw.wait()
    pl.semaphore_wait(barrier, tms - 1 + chips)

    halo_copy = pltpu.make_async_remote_copy(
        src_ref=raw_v.at[:, pl.ds(span - LANES, LANES)],
        dst_ref=halo,
        send_sem=halo_send,
        recv_sem=halo_recv,
        device_id=(c, jnp.minimum(z + 1, tms - 1)),
        device_id_type=MESH,
    )

    @pl.when(z < tms - 1)
    def _():
        halo_copy.start()

    @pl.when(z == 0)
    def _():
        halo[...] = jnp.zeros_like(halo)

    parts = span // WIDE
    stacked = jnp.concatenate([raw_v[:, q * WIDE : (q + 1) * WIDE] for q in range(parts)], axis=0)
    product = jnp.dot(
        stacked, table, precision=lax.Precision.HIGHEST, preferred_element_type=jnp.float32
    )
    step = WIDE // DECIM
    lane = lax.broadcasted_iota(jnp.int32, (rows, LANES), 1)
    total = product[:rows]
    for q in range(1, parts):
        turned = pltpu.roll(product[q * rows : (q + 1) * rows], q * step, 1)
        if q == parts - 1:
            turned = jnp.where(lane < DECIM, 0.0, turned)
        total = total + turned

    load_mask.wait()
    channels = rows * chans
    column = lax.broadcasted_iota(jnp.int32, weight_ref.shape, 1) // rows
    weight = jnp.zeros(weight_ref.shape, jnp.float32)
    for b in range(chans):
        weight = jnp.where(column == b, mask_ref[c, b].astype(jnp.float32), weight)
    weight_ref[...] = weight * (1.0 / math.sqrt(samples))

    @pl.when(z > 0)
    def _():
        halo_copy.wait_recv()

    before = jnp.dot(
        halo[...], table[WIDE - LANES :], precision=lax.Precision.HIGHEST,
        preferred_element_type=jnp.float32,
    )
    before = pltpu.roll(before, LANES - step, 1)
    total = total + jnp.where(lane < DECIM, before, 0.0)

    def rows_of(owner):
        return pl.ds(pl.multiple_of(owner * rows, rows), rows)

    record[z, rows_of(c)] = total.astype(jnp.bfloat16)

    def push(when, owner, target, send, recv):
        piece = record.at[when, rows_of(owner)]
        return pltpu.make_async_remote_copy(
            src_ref=piece, dst_ref=piece, send_sem=send, recv_sem=recv,
            device_id=target, device_id_type=MESH,
        )

    sent = []

    def start(copy):
        copy.start()
        sent.append(copy)

    def spread(when, slot):
        for d in range(1, chips):
            start(push(when, c, (c_peers[d - 1], z), c_send.at[d - 1, slot], c_recv.at[d - 1, slot]))
        start(push(when, c, (sibling, z), s_send.at[0, slot], s_recv.at[0, slot]))

    def relay(d, slot):
        when = z if slot == 0 else z_sources[slot - 1]
        owner = c_sources[d - 1]
        push(when, owner, (owner, z), c_send.at[d - 1, slot], c_recv.at[d - 1, slot]).wait_recv()
        start(push(when, owner, (sibling, z), s_send.at[d, slot], s_recv.at[d, slot]))

    for d in range(1, tms):
        start(push(z, c, (c, z_peers[d - 1]), z_send.at[d - 1], z_recv.at[d - 1]))
    spread(z, 0)
    for d in range(1, tms):
        source = z_sources[d - 1]
        push(source, c, (c, source), z_send.at[d - 1], z_recv.at[d - 1]).wait_recv()
        spread(source, d)
    for d in range(1, chips):
        relay(d, 0)

    def whiten_rows(owner):
        pieces = [record[k, rows_of(owner)].astype(jnp.float32) for k in range(tms)]
        whites = whiten(pieces, samples)
        for k, white in enumerate(whites):
            right[rows_of(owner), k * outputs : (k + 1) * outputs] = white
        return whites

    tiles = [white.astype(jnp.float32) for white in whiten_rows(c)]
    group = min(4, lag_count)

    def some_lags(turn, carry):
        for inner in range(group):
            number = turn * group + inner
            lag = z * lag_count + number
            earlier = jnp.zeros((rows, LANES), jnp.float32)
            for k, tile in enumerate(tiles):
                turned = pltpu.roll(tile, lag, 1)
                left[rows_of(number), k * LANES : (k + 1) * LANES] = jnp.where(
                    lane < lag, earlier, turned
                ).astype(jnp.bfloat16)
                earlier = turned
        return carry

    lax.fori_loop(0, lag_count // group, some_lags, 0)

    for slot in range(1, tms):
        for d in range(1, chips):
            relay(d, slot)
    for d in range(1, chips):
        whiten_rows(c_sources[d - 1])
    for d in range(chips):
        owner = sibling if d == 0 else c_sources[d - 1] + 1 - 2 * core
        for slot in range(tms):
            when = z if slot == 0 else z_sources[slot - 1]
            push(when, owner, (sibling, z), s_send.at[d, slot], s_recv.at[d, slot]).wait_recv()
        whiten_rows(owner)

    @pl.when(z < tms - 1)
    def _():
        halo_copy.wait_send()

    for copy in sent:
        copy.wait_send()


def correlate_kernel(left, right, weight_ref, out_hbm, out_v, sems):
    channels, samples = right.shape
    lag_count, rows = out_v.shape[:2]
    chunks = sems.shape[0]
    per = lag_count // chunks
    wide = min(channels, 512)
    copies = []
    for chunk in range(chunks):
        lags = pl.ds(chunk * per, per)

        def one(part, carry):
            at = pl.ds(pl.multiple_of(part * wide, wide), wide)
            product = lax.dot_general(
                left[chunk * per * rows : (chunk + 1) * per * rows], right[at],
                (((1,), (1,)), ((), ())), preferred_element_type=jnp.float32,
            )
            out_v[lags, :, at] = (product * weight_ref[0:1, at]).reshape(per, rows, wide)
            return carry

        if channels == wide:
            one(0, 0)
        else:
            lax.fori_loop(0, channels // wide, one, 0)
        copy = pltpu.make_async_copy(out_v.at[lags], out_hbm.at[lags], sems.at[chunk])
        copy.start()
        copies.append(copy)
    for copy in copies:
        copy.wait()


def per_device(raw_strain, fir_taps, block_mask, *, chans, tms):
    rows, span = raw_strain.shape
    outputs = span // DECIM
    samples = outputs * tms
    channels = rows * chans
    chips = chans // 2
    lag_count = LAGS // tms
    hbm = pl.BlockSpec(memory_space=pltpu.HBM)
    vmem = pl.BlockSpec(memory_space=pltpu.VMEM)
    dma = pltpu.SemaphoreType.DMA
    left, right, weight = pl.pallas_call(
        functools.partial(gather_kernel, chans, tms),
        out_shape=[
            jax.ShapeDtypeStruct((lag_count * rows, samples), jnp.bfloat16),
            jax.ShapeDtypeStruct((channels, samples), jnp.bfloat16),
            jax.ShapeDtypeStruct((8, channels), jnp.float32),
        ],
        in_specs=[hbm] * 3,
        out_specs=[vmem] * 3,
        scratch_shapes=[
            pltpu.VMEM((rows, span), jnp.float32),
            pltpu.SMEM((TAPS,), jnp.float32),
            pltpu.SMEM((chans, chans), jnp.int32),
            pltpu.VMEM((rows, LANES), jnp.float32),
            pltpu.VMEM((tms, channels, outputs), jnp.bfloat16),
            dma((3,)),
            dma,
            dma,
            dma((tms - 1,)),
            dma((tms - 1,)),
            dma((chips - 1, tms)),
            dma((chips - 1, tms)),
            dma((chips, tms)),
            dma((chips, tms)),
        ],
        compiler_params=pltpu.CompilerParams(
            collective_id=0, has_side_effects=True, vmem_limit_bytes=32 * 2**20
        ),
        name="gather",
    )(*[pltpu.with_memory_space_constraint(a, pltpu.HBM) for a in (fir_taps, raw_strain, block_mask)])

    chunks = min(8, lag_count)
    return pl.pallas_call(
        correlate_kernel,
        out_shape=jax.ShapeDtypeStruct((lag_count, rows, channels), jnp.float32),
        in_specs=[vmem] * 3,
        out_specs=hbm,
        scratch_shapes=[pltpu.VMEM((lag_count, rows, channels), jnp.float32), dma((chunks,))],
        compiler_params=pltpu.CompilerParams(vmem_limit_bytes=32 * 2**20),
        name="correlate",
    )(left, right, weight)


def solution(mesh):
    placed = (P("chan", "tm"), P(), P())
    return jax.shard_map(
        functools.partial(per_device, chans=mesh.shape["chan"], tms=mesh.shape["tm"]),
        mesh=mesh, in_specs=placed, out_specs=P("tm", "chan", None), check_vma=False,
    )
```

```python
import functools
import math

import jax
import jax.numpy as jnp
from jax import lax
from jax.experimental import pallas as pl
from jax.experimental.pallas import tpu as pltpu
from jax.sharding import PartitionSpec as P

DECIM = 8
TAPS = 64
LAGS = 128
LANES = 128
CUTS = 1
WIDE = 2 * LANES
MESH = pl.DeviceIdType.MESH


def filter_tile(taps_ref):
    row = lax.broadcasted_iota(jnp.int32, (DECIM, LANES), 0)
    lane = lax.broadcasted_iota(jnp.int32, (DECIM, LANES), 1)
    which = DECIM * lane + (DECIM - 1) - row
    base = jnp.zeros((DECIM, LANES), jnp.float32)
    for tap in range(TAPS):
        base = jnp.where(which == tap, taps_ref[tap], base)
    rows = [base if m == 0 else pltpu.roll(base, m, 1) for m in range(WIDE // DECIM)]
    return jnp.concatenate(rows, axis=0)


def flipped(index, bits):
    place = 1
    while place <= bits:
        if bits & place:
            index = index + place - 2 * place * lax.rem(index // place, 2)
        place *= 2
    return index


def whiten(pieces, samples):
    squares = pieces[0] * pieces[0]
    for piece in pieces[1:]:
        squares = squares + piece * piece
    root = jnp.sqrt(jnp.sum(squares, axis=1, keepdims=True) * (1.0 / samples) + 1e-06)
    return [(piece / root).astype(jnp.bfloat16) for piece in pieces]


def gather_kernel(
    chans, tms, taps_hbm, raw_hbm, mask_hbm, left, right, weight_ref,
    raw_v, taps_ref, mask_ref, ends, record,
    load_sems, e_send, e_recv, z_send, z_recv, c_send, c_recv, s_send, s_recv,
):
    rows, span = raw_v.shape
    outputs = span // DECIM
    samples = outputs * tms
    chips = chans // 2
    lag_count = left.shape[0] // rows
    c = lax.axis_index("chan")
    z = lax.axis_index("tm")
    chip, core = c // 2, lax.rem(c, 2)
    sibling = 2 * chip + (1 - core)

    load_raw = pltpu.make_async_copy(raw_hbm, raw_v, load_sems.at[0])
    load_taps = pltpu.make_async_copy(taps_hbm, taps_ref, load_sems.at[1])
    load_mask = pltpu.make_async_copy(mask_hbm, mask_ref, load_sems.at[2])
    load_taps.start()
    load_raw.start()
    load_mask.start()

    z_peers = [
        flipped(z, d) if tms & (tms - 1) == 0 else lax.rem(z + d, tms) for d in range(1, tms)
    ]
    z_sources = [
        flipped(z, d) if tms & (tms - 1) == 0 else lax.rem(z - d + tms, tms)
        for d in range(1, tms)
    ]
    power = chips & (chips - 1) == 0
    c_peers = [
        2 * (flipped(chip, d) if power else lax.rem(chip + d, chips)) + core
        for d in range(1, chips)
    ]
    c_sources = [
        2 * (flipped(chip, d) if power else lax.rem(chip - d + chips, chips)) + core
        for d in range(1, chips)
    ]
    barrier = pltpu.get_barrier_semaphore()
    for peer in z_peers:
        pl.semaphore_signal(barrier, inc=1, device_id=(c, peer), device_id_type=MESH)
    for peer in c_peers + [sibling]:
        pl.semaphore_signal(barrier, inc=1, device_id=(peer, z), device_id_type=MESH)

    load_taps.wait()
    table = filter_tile(taps_ref)
    load_raw.wait()

    parts = span // WIDE
    stacked = jnp.concatenate([raw_v[:, q * WIDE : (q + 1) * WIDE] for q in range(parts)], axis=0)
    product = jnp.dot(
        stacked, table, precision=lax.Precision.HIGHEST, preferred_element_type=jnp.float32
    )
    step = WIDE // DECIM
    lane = lax.broadcasted_iota(jnp.int32, (rows, LANES), 1)
    total = product[:rows]
    for q in range(1, parts):
        turned = pltpu.roll(product[q * rows : (q + 1) * rows], q * step, 1)
        if q == parts - 1:
            past = jnp.where(lane < DECIM, turned, 0.0)
            turned = jnp.where(lane < DECIM, 0.0, turned)
        total = total + turned

    record[z] = total.astype(jnp.bfloat16)
    both = jnp.where(lane < DECIM, total, jnp.where(lane < 2 * DECIM, pltpu.roll(past, DECIM, 1), 0.0))
    square = jnp.concatenate([both, jnp.zeros((LANES - rows, LANES), jnp.float32)], axis=0)
    ends[z] = square.T[: 2 * DECIM]

    def rows_of(owner):
        return pl.ds(pl.multiple_of(owner * rows, rows), rows)

    def share(ref, when, target, send, recv):
        return pltpu.make_async_remote_copy(
            src_ref=ref.at[when], dst_ref=ref.at[when], send_sem=send, recv_sem=recv,
            device_id=(c, target), device_id_type=MESH,
        )

    cut = rows // CUTS

    def push(owner, part, target, send, recv):
        piece = right.at[pl.ds(pl.multiple_of(owner * rows + part * cut, cut), cut)]
        return pltpu.make_async_remote_copy(
            src_ref=piece, dst_ref=piece, send_sem=send, recv_sem=recv,
            device_id=(target, z), device_id_type=MESH,
        )

    sent = []

    def start(copy):
        copy.start()
        sent.append(copy)

    pl.semaphore_wait(barrier, tms - 1 + chips)
    for d in reversed(range(1, tms)):
        start(share(ends, z, z_peers[d - 1], e_send.at[d - 1], e_recv.at[d - 1]))
        start(share(record, z, z_peers[d - 1], z_send.at[d - 1], z_recv.at[d - 1]))
    load_mask.wait()
    channels = rows * chans
    column = lax.broadcasted_iota(jnp.int32, weight_ref.shape, 1) // rows
    weight = jnp.zeros(weight_ref.shape, jnp.float32)
    for b in range(chans):
        weight = jnp.where(column == b, mask_ref[c, b].astype(jnp.float32), weight)
    weight_ref[...] = weight * (1.0 / math.sqrt(samples))

    for d in range(1, tms):
        source = z_sources[d - 1]
        share(ends, source, source, e_send.at[d - 1], e_recv.at[d - 1]).wait_recv()
        share(record, source, source, z_send.at[d - 1], z_recv.at[d - 1]).wait_recv()

    held = LANES // (2 * DECIM)
    turned_ends = []
    for base in range(0, tms, held):
        few = [ends[k] for k in range(base, min(base + held, tms))]
        short = LANES - 2 * DECIM * len(few)
        if short:
            few.append(jnp.zeros((short, LANES), jnp.float32))
        turned_ends.append(jnp.concatenate(few, axis=0).T[:rows])

    def end_of(k, tail):
        at = 2 * DECIM * (k % held) + DECIM * tail
        return pltpu.roll(turned_ends[k // held], (LANES - at) % LANES, 1)

    pieces = []
    for k in range(tms):
        edge = end_of(k, 0)
        if k:
            edge = edge + end_of(k - 1, 1)
        edge = edge.astype(jnp.bfloat16).astype(jnp.float32)
        pieces.append(jnp.where(lane < DECIM, edge, record[k].astype(jnp.float32)))
    whites = whiten(pieces, samples)
    for k, white in enumerate(whites):
        right[rows_of(c), k * outputs : (k + 1) * outputs] = white

    for part in range(CUTS):
        start(push(c, part, sibling, s_send.at[0, part], s_recv.at[0, part]))
    for part in range(CUTS):
        for d in reversed(range(1, chips)):
            start(push(c, part, c_peers[d - 1], c_send.at[d - 1, part], c_recv.at[d - 1, part]))

    tiles = [white.astype(jnp.float32) for white in whites]
    group = min(4, lag_count)

    def some_lags(turn, carry):
        for inner in range(group):
            number = turn * group + inner
            lag = z * lag_count + number
            earlier = jnp.zeros((rows, LANES), jnp.float32)
            for k, tile in enumerate(tiles):
                turned = pltpu.roll(tile, lag, 1)
                left[rows_of(number), k * LANES : (k + 1) * LANES] = jnp.where(
                    lane < lag, earlier, turned
                ).astype(jnp.bfloat16)
                earlier = turned
        return carry

    lax.fori_loop(0, lag_count // group, some_lags, 0)

    for part in range(CUTS):
        for d in range(1, chips):
            owner = c_sources[d - 1]
            push(owner, part, owner, c_send.at[d - 1, part], c_recv.at[d - 1, part]).wait_recv()
            start(push(owner, part, sibling, s_send.at[d, part], s_recv.at[d, part]))
    for part in range(CUTS):
        for d in range(chips):
            owner = sibling if d == 0 else c_sources[d - 1] + 1 - 2 * core
            push(owner, part, sibling, s_send.at[d, part], s_recv.at[d, part]).wait_recv()

    for copy in sent:
        copy.wait_send()


def correlate_kernel(left, right, weight_ref, out_hbm, out_v, sems):
    channels, samples = right.shape
    lag_count, rows = out_v.shape[:2]
    chunks = sems.shape[0]
    per = lag_count // chunks
    wide = min(channels, 512)
    copies = []
    for chunk in range(chunks):
        lags = pl.ds(chunk * per, per)

        def one(part, carry):
            at = pl.ds(pl.multiple_of(part * wide, wide), wide)
            product = lax.dot_general(
                left[chunk * per * rows : (chunk + 1) * per * rows], right[at],
                (((1,), (1,)), ((), ())), preferred_element_type=jnp.float32,
            )
            out_v[lags, :, at] = (product * weight_ref[0:1, at]).reshape(per, rows, wide)
            return carry

        if channels == wide:
            one(0, 0)
        else:
            lax.fori_loop(0, channels // wide, one, 0)
        copy = pltpu.make_async_copy(out_v.at[lags], out_hbm.at[lags], sems.at[chunk])
        copy.start()
        copies.append(copy)
    for copy in copies:
        copy.wait()


def per_device(raw_strain, fir_taps, block_mask, *, chans, tms):
    rows, span = raw_strain.shape
    outputs = span // DECIM
    samples = outputs * tms
    channels = rows * chans
    chips = chans // 2
    lag_count = LAGS // tms
    hbm = pl.BlockSpec(memory_space=pltpu.HBM)
    vmem = pl.BlockSpec(memory_space=pltpu.VMEM)
    dma = pltpu.SemaphoreType.DMA
    left, right, weight = pl.pallas_call(
        functools.partial(gather_kernel, chans, tms),
        out_shape=[
            jax.ShapeDtypeStruct((lag_count * rows, samples), jnp.bfloat16),
            jax.ShapeDtypeStruct((channels, samples), jnp.bfloat16),
            jax.ShapeDtypeStruct((8, channels), jnp.float32),
        ],
        in_specs=[hbm] * 3,
        out_specs=[vmem] * 3,
        scratch_shapes=[
            pltpu.VMEM((rows, span), jnp.float32),
            pltpu.SMEM((TAPS,), jnp.float32),
            pltpu.SMEM((chans, chans), jnp.int32),
            pltpu.VMEM((tms, 2 * DECIM, LANES), jnp.float32),
            pltpu.VMEM((tms, rows, outputs), jnp.bfloat16),
            dma((3,)),
            dma((tms - 1,)),
            dma((tms - 1,)),
            dma((tms - 1,)),
            dma((tms - 1,)),
            dma((chips - 1, CUTS)),
            dma((chips - 1, CUTS)),
            dma((chips, CUTS)),
            dma((chips, CUTS)),
        ],
        compiler_params=pltpu.CompilerParams(
            collective_id=0, has_side_effects=True, vmem_limit_bytes=32 * 2**20
        ),
        name="gather",
    )(*[pltpu.with_memory_space_constraint(a, pltpu.HBM) for a in (fir_taps, raw_strain, block_mask)])

    chunks = min(8, lag_count)
    return pl.pallas_call(
        correlate_kernel,
        out_shape=jax.ShapeDtypeStruct((lag_count, rows, channels), jnp.float32),
        in_specs=[vmem] * 3,
        out_specs=hbm,
        scratch_shapes=[pltpu.VMEM((lag_count, rows, channels), jnp.float32), dma((chunks,))],
        compiler_params=pltpu.CompilerParams(vmem_limit_bytes=32 * 2**20),
        name="correlate",
    )(left, right, weight)


def solution(mesh):
    placed = (P("chan", "tm"), P(), P())
    return jax.shard_map(
        functools.partial(per_device, chans=mesh.shape["chan"], tms=mesh.shape["tm"]),
        mesh=mesh, in_specs=placed, out_specs=P("tm", "chan", None), check_vma=False,
    )
```

```python
import functools
import math

import jax
import jax.numpy as jnp
from jax import lax
from jax.experimental import pallas as pl
from jax.experimental.pallas import tpu as pltpu
from jax.sharding import PartitionSpec as P

DECIM = 8
TAPS = 64
LAGS = 128
LANES = 128
CUTS = 1
WIDE = 2 * LANES
MESH = pl.DeviceIdType.MESH


def filter_tile(taps_ref):
    row = lax.broadcasted_iota(jnp.int32, (DECIM, LANES), 0)
    lane = lax.broadcasted_iota(jnp.int32, (DECIM, LANES), 1)
    which = DECIM * lane + (DECIM - 1) - row
    base = jnp.zeros((DECIM, LANES), jnp.float32)
    for tap in range(TAPS):
        base = jnp.where(which == tap, taps_ref[tap], base)
    rows = [base if m == 0 else pltpu.roll(base, m, 1) for m in range(WIDE // DECIM)]
    return jnp.concatenate(rows, axis=0)


def flipped(index, bits):
    place = 1
    while place <= bits:
        if bits & place:
            index = index + place - 2 * place * lax.rem(index // place, 2)
        place *= 2
    return index


def whiten(pieces, samples):
    squares = pieces[0] * pieces[0]
    for piece in pieces[1:]:
        squares = squares + piece * piece
    root = jnp.sqrt(jnp.sum(squares, axis=1, keepdims=True) * (1.0 / samples) + 1e-06)
    return [(piece / root).astype(jnp.bfloat16) for piece in pieces]


def gather_kernel(
    chans, tms, taps_hbm, raw_hbm, mask_hbm, left, right, weight_ref,
    raw_v, taps_ref, mask_ref, ends, record,
    load_sems, e_send, e_recv, z_send, z_recv, c_send, c_recv, s_send, s_recv,
):
    rows, span = raw_v.shape
    outputs = span // DECIM
    samples = outputs * tms
    chips = chans // 2
    lag_count = left.shape[0] // rows
    c = lax.axis_index("chan")
    z = lax.axis_index("tm")
    chip, core = c // 2, lax.rem(c, 2)
    sibling = 2 * chip + (1 - core)

    load_raw = pltpu.make_async_copy(raw_hbm, raw_v, load_sems.at[0])
    load_taps = pltpu.make_async_copy(taps_hbm, taps_ref, load_sems.at[1])
    load_mask = pltpu.make_async_copy(mask_hbm, mask_ref, load_sems.at[2])
    load_taps.start()
    load_raw.start()
    load_mask.start()

    z_peers = [
        flipped(z, d) if tms & (tms - 1) == 0 else lax.rem(z + d, tms) for d in range(1, tms)
    ]
    z_sources = [
        flipped(z, d) if tms & (tms - 1) == 0 else lax.rem(z - d + tms, tms)
        for d in range(1, tms)
    ]
    power = chips & (chips - 1) == 0
    c_peers = [
        2 * (flipped(chip, d) if power else lax.rem(chip + d, chips)) + core
        for d in range(1, chips)
    ]
    c_sources = [
        2 * (flipped(chip, d) if power else lax.rem(chip - d + chips, chips)) + core
        for d in range(1, chips)
    ]
    barrier = pltpu.get_barrier_semaphore()
    for peer in z_peers:
        pl.semaphore_signal(barrier, inc=1, device_id=(c, peer), device_id_type=MESH)
    for peer in c_peers + [sibling]:
        pl.semaphore_signal(barrier, inc=1, device_id=(peer, z), device_id_type=MESH)

    load_taps.wait()
    table = filter_tile(taps_ref)
    load_raw.wait()

    parts = span // WIDE
    stacked = jnp.concatenate([raw_v[:, q * WIDE : (q + 1) * WIDE] for q in range(parts)], axis=0)
    product = jnp.dot(
        stacked, table, precision=lax.Precision.HIGHEST, preferred_element_type=jnp.float32
    )
    step = WIDE // DECIM
    lane = lax.broadcasted_iota(jnp.int32, (rows, LANES), 1)
    total = product[:rows]
    for q in range(1, parts):
        turned = pltpu.roll(product[q * rows : (q + 1) * rows], q * step, 1)
        if q == parts - 1:
            past = jnp.where(lane < DECIM, turned, 0.0)
            turned = jnp.where(lane < DECIM, 0.0, turned)
        total = total + turned

    record[z] = total.astype(jnp.bfloat16)
    both = jnp.where(lane < DECIM, total, jnp.where(lane < 2 * DECIM, pltpu.roll(past, DECIM, 1), 0.0))
    square = jnp.concatenate([both, jnp.zeros((LANES - rows, LANES), jnp.float32)], axis=0)
    ends[z] = square.T[: 2 * DECIM]

    def rows_of(owner):
        return pl.ds(pl.multiple_of(owner * rows, rows), rows)

    def share(ref, when, target, send, recv):
        return pltpu.make_async_remote_copy(
            src_ref=ref.at[when], dst_ref=ref.at[when], send_sem=send, recv_sem=recv,
            device_id=(c, target), device_id_type=MESH,
        )

    cut = rows // CUTS

    def push(owner, part, target, send, recv):
        piece = right.at[pl.ds(pl.multiple_of(owner * rows + part * cut, cut), cut)]
        return pltpu.make_async_remote_copy(
            src_ref=piece, dst_ref=piece, send_sem=send, recv_sem=recv,
            device_id=(target, z), device_id_type=MESH,
        )

    sent = []

    def start(copy):
        copy.start()
        sent.append(copy)

    pl.semaphore_wait(barrier, tms - 1 + chips)
    for d in reversed(range(1, tms)):
        start(share(ends, z, z_peers[d - 1], e_send.at[d - 1], e_recv.at[d - 1]))
        start(share(record, z, z_peers[d - 1], z_send.at[d - 1], z_recv.at[d - 1]))
    load_mask.wait()
    channels = rows * chans
    column = lax.broadcasted_iota(jnp.int32, weight_ref.shape, 1) // rows
    weight = jnp.zeros(weight_ref.shape, jnp.float32)
    for b in range(chans):
        weight = jnp.where(column == b, mask_ref[c, b].astype(jnp.float32), weight)
    weight_ref[...] = weight * (1.0 / math.sqrt(samples))

    for d in range(1, tms):
        source = z_sources[d - 1]
        share(ends, source, source, e_send.at[d - 1], e_recv.at[d - 1]).wait_recv()
        share(record, source, source, z_send.at[d - 1], z_recv.at[d - 1]).wait_recv()

    held = LANES // (2 * DECIM)
    turned_ends = []
    for base in range(0, tms, held):
        few = [ends[k] for k in range(base, min(base + held, tms))]
        short = LANES - 2 * DECIM * len(few)
        if short:
            few.append(jnp.zeros((short, LANES), jnp.float32))
        turned_ends.append(jnp.concatenate(few, axis=0).T[:rows])

    def end_of(k, tail):
        at = 2 * DECIM * (k % held) + DECIM * tail
        return pltpu.roll(turned_ends[k // held], (LANES - at) % LANES, 1)

    pieces = []
    for k in range(tms):
        edge = end_of(k, 0)
        if k:
            edge = edge + end_of(k - 1, 1)
        edge = edge.astype(jnp.bfloat16).astype(jnp.float32)
        pieces.append(jnp.where(lane < DECIM, edge, record[k].astype(jnp.float32)))
    whites = whiten(pieces, samples)
    for k, white in enumerate(whites):
        right[rows_of(c), k * outputs : (k + 1) * outputs] = white

    for part in range(CUTS):
        start(push(c, part, sibling, s_send.at[0, part], s_recv.at[0, part]))
    for part in range(CUTS):
        for d in reversed(range(1, chips)):
            start(push(c, part, c_peers[d - 1], c_send.at[d - 1, part], c_recv.at[d - 1, part]))

    tiles = [white.astype(jnp.float32) for white in whites]
    group = min(4, lag_count)

    def some_lags(turn, carry):
        for inner in range(group):
            number = turn * group + inner
            lag = z * lag_count + number
            earlier = jnp.zeros((rows, LANES), jnp.float32)
            for k, tile in enumerate(tiles):
                turned = pltpu.roll(tile, lag, 1)
                left[rows_of(number), k * LANES : (k + 1) * LANES] = jnp.where(
                    lane < lag, earlier, turned
                ).astype(jnp.bfloat16)
                earlier = turned
        return carry

    lax.fori_loop(0, lag_count // group, some_lags, 0)

    for part in range(CUTS):
        for d in range(1, chips):
            owner = c_sources[d - 1]
            push(owner, part, owner, c_send.at[d - 1, part], c_recv.at[d - 1, part]).wait_recv()
            start(push(owner, part, sibling, s_send.at[d, part], s_recv.at[d, part]))
    for part in range(CUTS):
        for d in range(chips):
            owner = sibling if d == 0 else c_sources[d - 1] + 1 - 2 * core
            push(owner, part, sibling, s_send.at[d, part], s_recv.at[d, part]).wait_recv()

    for copy in sent:
        copy.wait_send()


def chunk_sizes(lag_count):
    sizes, done = [], 0
    while done < lag_count:
        sizes.append(min(max(1, done), 8, lag_count - done))
        done += sizes[-1]
    return sizes


def correlate_kernel(left, right, weight_ref, out_hbm, out_v, sems):
    channels, samples = right.shape
    lag_count, rows = out_v.shape[:2]
    wide = min(channels, 512)
    copies = []
    done = 0
    for chunk, per in enumerate(chunk_sizes(lag_count)):
        begin, done = done, done + per
        lags = pl.ds(begin, per)

        def one(part, carry):
            at = pl.ds(pl.multiple_of(part * wide, wide), wide)
            product = lax.dot_general(
                left[begin * rows : (begin + per) * rows], right[at],
                (((1,), (1,)), ((), ())), preferred_element_type=jnp.float32,
            )
            out_v[lags, :, at] = (product * weight_ref[0:1, at]).reshape(per, rows, wide)
            return carry

        if channels == wide:
            one(0, 0)
        else:
            lax.fori_loop(0, channels // wide, one, 0)
        copy = pltpu.make_async_copy(out_v.at[lags], out_hbm.at[lags], sems.at[chunk])
        copy.start()
        copies.append(copy)
    for copy in copies:
        copy.wait()


def per_device(raw_strain, fir_taps, block_mask, *, chans, tms):
    rows, span = raw_strain.shape
    outputs = span // DECIM
    samples = outputs * tms
    channels = rows * chans
    chips = chans // 2
    lag_count = LAGS // tms
    hbm = pl.BlockSpec(memory_space=pltpu.HBM)
    vmem = pl.BlockSpec(memory_space=pltpu.VMEM)
    dma = pltpu.SemaphoreType.DMA
    left, right, weight = pl.pallas_call(
        functools.partial(gather_kernel, chans, tms),
        out_shape=[
            jax.ShapeDtypeStruct((lag_count * rows, samples), jnp.bfloat16),
            jax.ShapeDtypeStruct((channels, samples), jnp.bfloat16),
            jax.ShapeDtypeStruct((8, channels), jnp.float32),
        ],
        in_specs=[hbm] * 3,
        out_specs=[vmem] * 3,
        scratch_shapes=[
            pltpu.VMEM((rows, span), jnp.float32),
            pltpu.SMEM((TAPS,), jnp.float32),
            pltpu.SMEM((chans, chans), jnp.int32),
            pltpu.VMEM((tms, 2 * DECIM, LANES), jnp.float32),
            pltpu.VMEM((tms, rows, outputs), jnp.bfloat16),
            dma((3,)),
            dma((tms - 1,)),
            dma((tms - 1,)),
            dma((tms - 1,)),
            dma((tms - 1,)),
            dma((chips - 1, CUTS)),
            dma((chips - 1, CUTS)),
            dma((chips, CUTS)),
            dma((chips, CUTS)),
        ],
        compiler_params=pltpu.CompilerParams(
            collective_id=0, has_side_effects=True, vmem_limit_bytes=32 * 2**20
        ),
        name="gather",
    )(*[pltpu.with_memory_space_constraint(a, pltpu.HBM) for a in (fir_taps, raw_strain, block_mask)])

    chunks = len(chunk_sizes(lag_count))
    return pl.pallas_call(
        correlate_kernel,
        out_shape=jax.ShapeDtypeStruct((lag_count, rows, channels), jnp.float32),
        in_specs=[vmem] * 3,
        out_specs=hbm,
        scratch_shapes=[pltpu.VMEM((lag_count, rows, channels), jnp.float32), dma((chunks,))],
        compiler_params=pltpu.CompilerParams(vmem_limit_bytes=32 * 2**20),
        name="correlate",
    )(left, right, weight)


def solution(mesh):
    placed = (P("chan", "tm"), P(), P())
    return jax.shard_map(
        functools.partial(per_device, chans=mesh.shape["chan"], tms=mesh.shape["tm"]),
        mesh=mesh, in_specs=placed, out_specs=P("tm", "chan", None), check_vma=False,
    )
```
